32 devices in a mesh: groups: 2 (over x), ctx: 16 (over z, y, core).
Axes of the slice: x: 2, y: 2, z: 4, core: 2. Of those that a mesh axis runs over, the one named last changes fastest.
Arguments:
- queries: bfloat16 [32, 384, 512], P(('groups', 'ctx')), parts along dimension 0
- span_kv: bfloat16 [32, 2, 384, 512], P(('groups', 'ctx')), parts along dimension 0
- prefix_pool: bfloat16 [32, 4, 2, 128, 512], P(('groups', 'ctx')), parts along dimension 0, may hold values from -6 to 6
- token_pos: int32 [3072], P('groups'), parts along dimension 0, may hold values from 0 to 1535, as said below
- span_lens: int32 [8], P('groups'), parts along dimension 0, may hold values from 1 to 768, 1536 in all
- prefix_lens: int32 [8], P('groups'), parts along dimension 0, may hold values from 64 to 512, as said below
- block_table: int32 [8, 4, 2], P('groups'), parts along dimension 0, may hold values from 0 to 3, as said below
Outputs:
- attended: bfloat16 [32, 384, 512], P(('groups', 'ctx')), parts along dimension 0
The draws below stay inside these ranges and needn't reach their ends.
There are 2 independent parts, one for each index of `groups`. The reference program is written for one: setup_inputs(seed, part) draws one part's arguments, and reference() takes and returns one part's arrays. A program takes and returns all parts, laid end to end along the dimension named above; each array names one. Nothing has to cross between parts.
Inputs may be any that keep to these rules, and one draw needn't show every extreme that they name: `token_pos`: position block s holds pieces p and 7 - p of length 384 // 2 (rows of the first piece first), for a permutation p of the blocks drawn from the seed. `span_lens`: the lengths sum to 1536; the longest is exactly 768. `prefix_lens`: one request has exactly 512 cached tokens. `block_table`: every pair of pool block and slot appears exactly once in the table.
All inputs are finite; a program needn't handle non-finite values.
Results may differ from the reference program's by a relative error of at most 0.0055.
Values may be sent and summed in bfloat16 or wider, within the bound.
No kernel may reach another device: no remote copies, remote signals or barrier semaphores. Data moves between devices by JAX's collectives and lax.ppermute only.
A program may use at most 64 MiB of HBM per device.

```python
import math
import jax
import jax.numpy as jnp
import numpy as np
from jax import lax

HEADS = 16
HEAD_DIM = 128
HGROUPS = 4
BLK = 128
SLOTS = 4
REQS = 4
TOK_DEV = 384
NSEQ = 4
SLABS = 16
FEAT = 512
SPAN = 1536
MAXBLK = 4


def base_keys(key):
    return jax.random.normal(key, (SLABS, TOK_DEV, FEAT), jnp.float32)


def draw_queries(key, part):
    key = jax.random.fold_in(key, 1)
    fresh = jax.random.normal(key, (SLABS, TOK_DEV, FEAT), jnp.float32)
    return fresh.astype(jnp.bfloat16)


def draw_span_kv(key, part):
    common = base_keys(key)
    key = jax.random.fold_in(key, 3)
    keys = common
    values = jax.random.normal(key, (SLABS, TOK_DEV, FEAT), jnp.float32)
    return jnp.stack([keys, values], axis=1).astype(jnp.bfloat16)


def draw_token_pos(key, part):
    key = jax.random.fold_in(key, 21)
    order = jax.random.permutation(key, NSEQ)
    half = TOK_DEV // 2
    row = jnp.arange(TOK_DEV)
    first = order[:, None] * half + row[None, :]
    second = (2 * NSEQ - 1 - order)[:, None] * half + row[None, :] - half
    return jnp.where(row[None, :] < half, first, second).reshape(-1).astype(jnp.int32)


def draw_prefix_lens(key, part):
    key = jax.random.fold_in(key, 7)
    most = MAXBLK * BLK
    lens = jax.random.randint(key, (REQS,), BLK // 2, most + 1)
    which = jax.random.randint(jax.random.fold_in(key, 8), (), 0, REQS)
    return jnp.where(jnp.arange(REQS) == which, most, lens).astype(jnp.int32)


def draw_block_table(key, part):
    key = jax.random.fold_in(key, 9)
    order = jax.random.permutation(key, NSEQ * SLOTS).reshape(REQS, MAXBLK)
    return jnp.stack([order // SLOTS, order % SLOTS], axis=-1).astype(jnp.int32)


def level_of(stream_key, extent, pieces, smallest, largest):
    gain, own = 1.0, jax.random.fold_in(stream_key, 6)
    for dim, parts in pieces:
        draws = jnp.exp(jax.random.uniform(jax.random.fold_in(own, dim), (parts,), jnp.float32, smallest / len(pieces), largest / len(pieces)))
        gain = gain * jnp.repeat(draws, extent[dim] // parts).reshape([-1 if axis == dim else 1 for axis in range(len(extent))])
    return gain


def split_up(number_of, total, reach, skew):
    portions = [(1 << 20) // math.isqrt(rank ** skew) + 1 for rank in range(2, number_of + 1)]
    surplus, counts = total - reach - (number_of - 1), [1] * (number_of - 1)
    while surplus > 0:
        movable = [i for i in range(number_of - 1) if counts[i] < reach]
        mass, budget = sum([portions[i] for i in movable]), surplus
        for i in movable:
            addition = min(reach - counts[i], max(1, budget * portions[i] // mass), surplus)
            counts[i] = counts[i] + addition
            surplus = surplus - addition
    return np.array([reach] + counts)


def ragged(stream_key, count, total, bound, slope):
    if count == 2:
        one = jax.random.randint(stream_key, (), max(1, total - bound), min(bound, total - 1) + 1)
        return jnp.stack([one, total - one])
    tallies = jnp.asarray(split_up(count, total, bound, slope), jnp.int32)
    couples = (count - 1) // 2
    donor, taker = tallies[1:1 + 2 * couples:2], tallies[2:2 + 2 * couples:2]
    margin = jnp.minimum(donor - 1, bound - taker)
    shifted = jax.random.randint(jax.random.fold_in(stream_key, 1), (couples,), 0, 1 << 20) % (margin + 1)
    tallies = tallies.at[1:1 + 2 * couples:2].set(donor - shifted).at[2:2 + 2 * couples:2].set(taker + shifted)
    return tallies[jax.random.permutation(jax.random.fold_in(stream_key, 2), count)]


def noise(key, shape, deviation, most, pieces=(), held_as=jnp.bfloat16):
    level = level_of(key, shape, pieces, -0.22, 0.18) if pieces else 1.0
    values = jax.random.normal(key, shape, jnp.float32) * deviation * level
    return jnp.minimum(jnp.maximum(values, -most), most).astype(held_as)


def setup_inputs(seed: int = 0, part: int = 0) -> dict:
    splits = jax.random.split(jax.random.key(seed), 8)
    own_keys = jax.random.split(jax.random.fold_in(splits[7], part), 8)
    queries = draw_queries(jax.random.fold_in(jax.random.fold_in(splits[7], part), 71), part)
    span_kv = draw_span_kv(jax.random.fold_in(jax.random.fold_in(splits[7], part), 71), part)
    prefix_pool = noise(own_keys[2], (SLABS, SLOTS, 2, BLK, FEAT), 1.0, 6.0, ((0, 16),))
    token_pos = draw_token_pos(jax.random.fold_in(jax.random.fold_in(splits[7], part), 71), part)
    span_lens = ragged(own_keys[4], REQS, SPAN, SPAN // 2, 1).astype(jnp.int32)
    prefix_lens = draw_prefix_lens(jax.random.fold_in(jax.random.fold_in(splits[7], part), 71), part)
    block_table = draw_block_table(jax.random.fold_in(jax.random.fold_in(splits[7], part), 71), part)
    return {"queries": queries, "span_kv": span_kv, "prefix_pool": prefix_pool, "token_pos": token_pos, "span_lens": span_lens, "prefix_lens": prefix_lens, "block_table": block_table}


def request_of(positions, ends):
    return lax.optimization_barrier(jnp.sum((positions[:, None] >= ends[None, :]).astype(jnp.int32), axis=1))

def slot_owners(block_table, prefix_lens, total_slots):
    reqs = block_table.shape[0]
    most = block_table.shape[1]
    ids = (block_table[:, :, 0] * SLOTS + block_table[:, :, 1]).reshape(-1)
    req_index = (jnp.arange(reqs, dtype=jnp.int32)[:, None] + jnp.zeros((1, most), jnp.int32)).reshape(-1)
    blk_index = (jnp.zeros((reqs, 1), jnp.int32) + jnp.arange(most, dtype=jnp.int32)[None, :]).reshape(-1)
    every = jnp.arange(total_slots, dtype=jnp.int32)
    match = ids[:, None] == every[None, :]
    owner = lax.optimization_barrier(jnp.sum(jnp.where(match, req_index[:, None], 0), axis=0)).astype(jnp.int32)
    first = lax.optimization_barrier(jnp.sum(jnp.where(match, blk_index[:, None] * BLK, 0), axis=0)).astype(jnp.int32)
    own_len = lax.optimization_barrier(jnp.sum(jnp.where(owner[:, None] == jnp.arange(reqs, dtype=jnp.int32)[None, :], prefix_lens[None, :], 0), axis=1))
    valid = jnp.clip(own_len - first, 0, BLK).astype(jnp.int32)
    return (owner, valid)

def reference(queries, span_kv, prefix_pool, token_pos, span_lens, prefix_lens, block_table):
    split = HEADS // HGROUPS
    scale = 1.0 / math.sqrt(HEAD_DIM)
    q_all = queries.reshape(NSEQ, HGROUPS, TOK_DEV, split, HEAD_DIM).transpose(1, 3, 0, 2, 4).reshape(HEADS, SPAN, HEAD_DIM)
    kv_all = span_kv.reshape(NSEQ, HGROUPS, 2, TOK_DEV, split, HEAD_DIM).transpose(2, 1, 4, 0, 3, 5).reshape(2, HEADS, SPAN, HEAD_DIM)
    pooled = prefix_pool.reshape(NSEQ, HGROUPS, SLOTS, 2, BLK, split, HEAD_DIM).transpose(3, 1, 5, 0, 2, 4, 6).reshape(2, HEADS, NSEQ * SLOTS * BLK, HEAD_DIM)
    keys = jnp.concatenate([kv_all[0], pooled[0]], axis=1)
    values = jnp.concatenate([kv_all[1], pooled[1]], axis=1)
    ends = jnp.cumsum(span_lens)
    req = request_of(token_pos, ends)
    span_mask = (req[:, None] == req[None, :]) & (token_pos[None, :] <= token_pos[:, None])
    owner, valid = slot_owners(block_table, prefix_lens, NSEQ * SLOTS)
    key_req = jnp.repeat(owner, BLK)
    live = (jnp.arange(BLK, dtype=jnp.int32)[None, :] < valid[:, None]).reshape(-1)
    pool_mask = (req[:, None] == key_req[None, :]) & live[None, :]
    mask = jnp.concatenate([span_mask, pool_mask], axis=1)

    def one_head(operands):
        q_head, k_head, v_head = operands
        scores = jnp.dot(q_head, k_head.T, preferred_element_type=jnp.float32) * scale
        scores = jnp.where(mask, scores, -jnp.inf)
        peak = lax.optimization_barrier(jnp.max(scores, axis=1, keepdims=True))
        weights = jnp.where(mask, jnp.exp(scores - peak), 0.0)
        total = lax.optimization_barrier(jnp.sum(weights, axis=1, keepdims=True))
        return jnp.dot(weights.astype(jnp.bfloat16), v_head, preferred_element_type=jnp.float32) / total
    result = lax.map(one_head, (q_all, keys, values))
    result = result.reshape(HGROUPS, split, NSEQ, TOK_DEV, HEAD_DIM).transpose(2, 0, 3, 1, 4)
    return result.reshape(NSEQ * HGROUPS, TOK_DEV, split * HEAD_DIM).astype(jnp.bfloat16)
```

```python
import functools
import math

import jax
import jax.numpy as jnp
from jax import lax
from jax.experimental import pallas as pl
from jax.experimental.pallas import tpu as pltpu
from jax.sharding import PartitionSpec as P

HEAD_DIM = 128
HGROUPS = 4
TILE = 128
TAIL = 16
FLOOR = -(2.0**126)
LOWEST = float(jnp.finfo(jnp.float32).min)
LOG2E = 1.4426950408889634


def hop(value, axis, count, right, first, last):
    step = 1 if right else -1
    pairs = [
        (block * HGROUPS + group, (block + step) * HGROUPS + group)
        for block in range(first, last)
        for group in range(HGROUPS)
    ]
    return lax.ppermute(value, axis, pairs)


class Layout:
    def __init__(self, reqs, slots, count):
        self.ends = 0
        self.low = self.ends + reqs
        self.high = self.low + slots
        self.valid = self.high + slots
        self.first = self.valid + slots
        self.second = self.first + count
        self.me = self.second + count
        self.size = self.me + 1
        self.reqs, self.slots, self.count = reqs, slots, count


def start_of(table, lay, pos):
    start = jnp.zeros_like(pos)
    for r in range(lay.reqs - 1):
        end = table[lay.ends + r]
        start = jnp.where(pos >= end, end, start)
    return start


def attend(table, lay, rows, heads, source, chunk, query_of, key_of, value_of, me, scale, peak, total, accum):
    half = rows // 2
    lane0 = chunk * TILE
    base1, base2 = table[lay.first + source], table[lay.second + source] - half
    lane = lane0 + lax.broadcasted_iota(jnp.int32, (1, TILE), 1)
    pos = jnp.where(lane < half, base1, base2) + lane
    start = start_of(table, lay, pos)
    pieces = []
    for low, high, base in ((0, half, base1), (half, rows, base2)):
        low, high = max(low, lane0), min(high, lane0 + TILE)
        if low < high:
            pieces.append((base + low, base + high))
    needed = [(start_of(table, lay, low), high) for low, high in pieces]
    peak[...] = jnp.full_like(peak, LOWEST)
    total[...] = jnp.zeros_like(total)
    accum[...] = jnp.zeros_like(accum)

    def tile(index, visible):
        for h in range(heads):
            cols = slice(h * HEAD_DIM, (h + 1) * HEAD_DIM)
            scores = lax.dot_general(
                key_of(index, cols), query_of(cols), (((1,), (1,)), ((), ())), preferred_element_type=jnp.float32
            )
            scores = jnp.where(visible, scores * scale, -jnp.inf)
            old = peak[h : h + 1]
            fresh = jnp.maximum(old, jnp.max(scores, axis=0, keepdims=True))
            weights = jnp.exp2(scores - fresh)
            factor = jnp.exp2(old - fresh)
            peak[h : h + 1] = fresh
            total[h : h + 1] = total[h : h + 1] * factor + jnp.sum(weights, axis=0, keepdims=True)
            accum[cols] = accum[cols] * factor + jnp.dot(
                value_of(index, cols), weights.astype(jnp.bfloat16), preferred_element_type=jnp.float32
            )

    down = lax.broadcasted_iota(jnp.int32, (TILE, TILE), 0)
    own1, own2 = table[lay.first + me], table[lay.second + me] - half
    for t in range(rows // TILE):
        spans = []
        for low, high, base in ((0, half, own1), (half, rows, own2)):
            low, high = max(low, t * TILE), min(high, (t + 1) * TILE)
            if low < high:
                spans.append((base + low, base + high))
        used = False
        for low, high in needed:
            for key_low, key_high in spans:
                used = used | ((low < key_high) & (key_low < high))

        @pl.when(used)
        def _():
            if (t + 1) * TILE <= half:
                key_pos = down + (own1 + t * TILE)
            elif t * TILE >= half:
                key_pos = down + (own2 + t * TILE)
            else:
                key_pos = down + t * TILE
                key_pos = key_pos + jnp.where(key_pos < half, own1, own2)
            tile(t, (key_pos <= pos) & (key_pos >= start))

    for slot in range(lay.slots):
        low, high, live = table[lay.low + slot], table[lay.high + slot], table[lay.valid + slot]
        used = False
        for first, last in pieces:
            used = used | ((first < high) & (low < last))

        @pl.when(used & (live > 0))
        def _():
            limit = jnp.where((pos >= low) & (pos < high), live, 0)
            tile(rows // TILE + slot, down < limit)


def settle(heads, peak, total, accum, out):
    sums = total[:heads]
    empty = sums == 0.0
    safe = jnp.where(empty, 1.0, sums)
    level = jnp.where(empty, FLOOR, peak[:heads] + jnp.log2(safe))
    inverse = 1.0 / safe
    feat = heads * HEAD_DIM
    for h in range(heads):
        cols = slice(h * HEAD_DIM, (h + 1) * HEAD_DIM)
        out[cols] = accum[cols] * inverse[h : h + 1]
    out[feat : feat + heads] = level
    out[feat + heads :] = jnp.zeros_like(out[feat + heads :])


def first_kernel(lay, rows, heads, scale, me_ref, pos_ref, span_len, prefix_len, blocks, queries, span, pool, table, keys, values, own, peak, total, accum):
    me = me_ref[0]
    reqs, most = blocks.shape[0], blocks.shape[1]
    width = pool.shape[2]
    begins, end = [], 0
    for r in range(reqs):
        begins.append(end)
        end = end + span_len[r]
        table[lay.ends + r] = end
    for b in range(lay.count):
        table[lay.first + b] = pos_ref[b * rows]
        table[lay.second + b] = pos_ref[b * rows + rows // 2]
    table[lay.me] = me
    for r in range(reqs):
        for b in range(most):

            @pl.when(blocks[r, b, 0] == me)
            def _():
                slot = blocks[r, b, 1]
                table[lay.low + slot] = begins[r] + jnp.int32(0)
                table[lay.high + slot] = table[lay.ends + r]
                table[lay.valid + slot] = jnp.clip(prefix_len[r] - b * width, 0, width)

    tiles = rows // TILE
    for t in range(tiles):
        keys[t] = span[0, t * TILE : (t + 1) * TILE]
        for h in range(heads):
            cols = slice(h * HEAD_DIM, (h + 1) * HEAD_DIM)
            values[t, cols] = span[1, t * TILE : (t + 1) * TILE, cols].T
    for slot in range(lay.slots):
        keys[tiles + slot] = pool[slot, 0]
        for h in range(heads):
            cols = slice(h * HEAD_DIM, (h + 1) * HEAD_DIM)
            values[tiles + slot, cols] = pool[slot, 1, :, cols].T
    for c in range(tiles):
        attend(
            table, lay, rows, heads, me, c,
            lambda cols: queries[c * TILE : (c + 1) * TILE, cols],
            lambda t, cols: keys[t, :, cols],
            lambda t, cols: values[t, cols],
            me, scale, peak, total, accum,
        )
        settle(heads, peak, total, accum, own.at[c])


def partial_kernel(lay, rows, heads, scale, chunk, distance, table, from_left, from_right, keys, values, part_left, part_right, peak, total, accum):
    me = table[lay.me]
    for query, part, source in (
        (from_left, part_left, me - distance),
        (from_right, part_right, me + distance),
    ):

        @pl.when((source >= 0) & (source < lay.count))
        def _():
            attend(
                table, lay, rows, heads, source, chunk,
                lambda cols: query[:, cols],
                lambda t, cols: keys[t, :, cols],
                lambda t, cols: values[t, cols],
                me, scale, peak, total, accum,
            )
            settle(heads, peak, total, accum, part)


def level_of(item, feat, heads):
    tail = item[feat : feat + TAIL].astype(jnp.float32)
    return tail[:heads] + tail[heads : 2 * heads] + tail[2 * heads : 3 * heads]


def put_level(item, feat, heads, level):
    high = level.astype(jnp.bfloat16).astype(jnp.float32)
    rest = level - high
    middle = rest.astype(jnp.bfloat16).astype(jnp.float32)
    parts = [high, middle, rest - middle, jnp.zeros((TAIL - 3 * heads, TILE), jnp.float32)]
    item[feat : feat + TAIL] = jnp.concatenate(parts, axis=0).astype(jnp.bfloat16)


def merge_kernel(lay, heads, distance, table, part_left, part_right, *refs):
    me = table[lay.me]
    feat = heads * HEAD_DIM
    if len(refs) == 2:
        got_left = got_right = None
        item_left, item_right = refs
    else:
        got_left, got_right, item_left, item_right = refs
    for part, got, item, has, more in (
        (part_left, got_left, item_left, me - distance >= 0, me + 1 < lay.count),
        (part_right, got_right, item_right, me + distance < lay.count, me > 0),
    ):

        @pl.when(has & jnp.logical_not(more) if got is not None else has)
        def _():
            item[:feat] = part[:feat].astype(jnp.bfloat16)
            put_level(item, feat, heads, part[feat : feat + heads])

        if got is not None:

            @pl.when(has & more)
            def _():
                mine = part[feat : feat + heads]
                theirs = level_of(got, feat, heads)
                top = jnp.maximum(mine, theirs)
                level = top + jnp.log2(jnp.exp2(mine - top) + jnp.exp2(theirs - top))
                a, b = jnp.exp2(mine - level), jnp.exp2(theirs - level)
                for h in range(heads):
                    cols = slice(h * HEAD_DIM, (h + 1) * HEAD_DIM)
                    item[cols] = (
                        part[cols] * a[h : h + 1] + got[cols].astype(jnp.float32) * b[h : h + 1]
                    ).astype(jnp.bfloat16)
                put_level(item, feat, heads, level)


def last_kernel(lay, heads, table, part, got_left, got_right, whole, out):
    me = table[lay.me]
    feat = heads * HEAD_DIM
    own = part[feat : feat + heads]
    left = jnp.where(me > 0, level_of(got_left, feat, heads), FLOOR)
    right = jnp.where(me + 1 < lay.count, level_of(got_right, feat, heads), FLOOR)
    top = jnp.maximum(own, jnp.maximum(left, right))
    shares = [jnp.exp2(level - top) for level in (own, left, right)]
    inverse = 1.0 / (shares[0] + shares[1] + shares[2])
    a, b, c = (share * inverse for share in shares)
    for h in range(heads):
        cols = slice(h * HEAD_DIM, (h + 1) * HEAD_DIM)
        value = part[cols] * a[h : h + 1]
        value = value + got_left[cols].astype(jnp.float32) * b[h : h + 1]
        value = value + got_right[cols].astype(jnp.float32) * c[h : h + 1]
        out[0, :, cols] = value.T.astype(jnp.bfloat16)


def shards(queries, span_kv, prefix_pool, token_pos, span_lens, prefix_lens, block_table):
    rows, feat = queries.shape[1], queries.shape[2]
    heads = feat // HEAD_DIM
    count = lax.axis_size("ctx") // HGROUPS
    slots, width = prefix_pool.shape[1], prefix_pool.shape[3]
    assert width == TILE and rows % TILE == 0
    chunks = rows // TILE
    tiles = chunks + slots
    scale = LOG2E / math.sqrt(HEAD_DIM)
    lay = Layout(span_lens.shape[0], slots, count)
    me = (lax.axis_index("ctx") // HGROUPS).reshape(1)

    smem = pl.BlockSpec(memory_space=pltpu.SMEM)
    vmem = pl.BlockSpec(memory_space=pltpu.VMEM)
    part_rows = feat + 8
    part_shape = jax.ShapeDtypeStruct((part_rows, TILE), jnp.float32)
    item_shape = jax.ShapeDtypeStruct((feat + TAIL, TILE), jnp.bfloat16)
    state = [
        pltpu.VMEM((8, TILE), jnp.float32),
        pltpu.VMEM((8, TILE), jnp.float32),
        pltpu.VMEM((feat, TILE), jnp.float32),
    ]
    params = pltpu.CompilerParams(vmem_limit_bytes=24 * 1024 * 1024)

    def cost(blocks):
        return pl.CostEstimate(
            flops=blocks * 4 * TILE * tiles * TILE * feat, bytes_accessed=tiles * 4 * TILE * feat, transcendentals=blocks * tiles * TILE * TILE * heads
        )

    table, keys, values, own = pl.pallas_call(
        functools.partial(first_kernel, lay, rows, heads, scale),
        out_shape=(
            jax.ShapeDtypeStruct((lay.size,), jnp.int32),
            jax.ShapeDtypeStruct((tiles, TILE, feat), jnp.bfloat16),
            jax.ShapeDtypeStruct((tiles, feat, TILE), jnp.bfloat16),
            jax.ShapeDtypeStruct((chunks, part_rows, TILE), jnp.float32),
        ),
        in_specs=[smem] * 5 + [vmem] * 3,
        out_specs=(smem, vmem, vmem, vmem),
        scratch_shapes=state,
        compiler_params=params,
        cost_estimate=cost(chunks),
        name="own_part",
    )(me, token_pos, span_lens, prefix_lens, block_table, queries[0], span_kv[0], prefix_pool[0])

    from_left = [[queries[0, c * TILE : (c + 1) * TILE]] for c in range(chunks)]
    from_right = [[queries[0, c * TILE : (c + 1) * TILE]] for c in range(chunks)]
    for d in range(1, count):
        for c in range(chunks):
            from_left[c].append(hop(from_left[c][-1], "ctx", count, True, d - 1, count - 1))
            from_right[c].append(hop(from_right[c][-1], "ctx", count, False, 1, count - d + 1))

    out = jnp.zeros((1, rows, feat), jnp.bfloat16)
    for c in range(chunks):
        got_left = got_right = None
        for d in range(count - 1, 0, -1):
            parts = pl.pallas_call(
                functools.partial(partial_kernel, lay, rows, heads, scale, c, d),
                out_shape=(part_shape, part_shape),
                in_specs=[smem] + [vmem] * 4,
                out_specs=(vmem, vmem),
                scratch_shapes=state,
                compiler_params=params,
                cost_estimate=cost(1),
                name="part",
            )(table, from_left[c][d], from_right[c][d], keys, values)
            got = () if got_left is None else (got_right, got_left)
            items = pl.pallas_call(
                functools.partial(merge_kernel, lay, heads, d),
                out_shape=(item_shape, item_shape),
                in_specs=[smem] + [vmem] * (2 + len(got)),
                out_specs=(vmem, vmem),
                compiler_params=params,
                cost_estimate=pl.CostEstimate(flops=4 * TILE * feat, bytes_accessed=12 * TILE * feat, transcendentals=0),
                name="merge",
            )(table, *parts, *got)
            got_right = hop(items[0], "ctx", count, False, d, count)
            got_left = hop(items[1], "ctx", count, True, 0, count - d)
        out = pl.pallas_call(
            functools.partial(last_kernel, lay, heads),
            out_shape=jax.ShapeDtypeStruct(out.shape, out.dtype),
            grid=(1,),
            in_specs=[
                smem,
                pl.BlockSpec((None, part_rows, TILE), lambda i, c=c: (c, 0, 0)),
                pl.BlockSpec(item_shape.shape, lambda i: (0, 0)),
                pl.BlockSpec(item_shape.shape, lambda i: (0, 0)),
                pl.BlockSpec(memory_space=pl.ANY),
            ],
            out_specs=pl.BlockSpec((1, TILE, feat), lambda i, c=c: (0, c, 0)),
            input_output_aliases={4: 0},
            compiler_params=params,
            cost_estimate=pl.CostEstimate(flops=4 * TILE * feat, bytes_accessed=12 * TILE * feat, transcendentals=0),
            name="last",
        )(table, own, got_left, got_right, out)
    return out


def solution(mesh):
    placed = (
        P(("groups", "ctx"), None, None),
        P(("groups", "ctx"), None, None, None),
        P(("groups", "ctx"), None, None, None, None),
        P("groups"),
        P("groups"),
        P("groups"),
        P("groups", None, None),
    )
    return jax.shard_map(
        shards,
        mesh=mesh,
        in_specs=placed,
        out_specs=P(("groups", "ctx"), None, None),
        check_vma=False,
    )
```

```python
import functools
import math

import jax
import jax.numpy as jnp
from jax import lax
from jax.experimental import pallas as pl
from jax.experimental.pallas import tpu as pltpu
from jax.sharding import PartitionSpec as P

HEAD_DIM = 128
HGROUPS = 4
TILE = 128
TAIL = 16
FLOOR = -(2.0**126)
LOWEST = float(jnp.finfo(jnp.float32).min)
LOG2E = 1.4426950408889634


def send(value, target_of, count):
    pairs = [
        (block * HGROUPS + group, target_of(block) * HGROUPS + group)
        for block in range(count)
        for group in range(HGROUPS)
        if target_of(block) is not None
    ]
    return lax.ppermute(value, "ctx", pairs)


class Layout:
    def __init__(self, reqs, rows, slots, count):
        self.reqs, self.rows, self.slots, self.count = reqs, rows, slots, count
        self.chunks = rows // TILE
        self.tiles = self.chunks + slots
        self.ends = 0
        self.low = self.ends + reqs
        self.high = self.low + self.tiles
        self.low2 = self.high + self.tiles
        self.high2 = self.low2 + self.tiles
        self.valid = self.high2 + self.tiles
        self.first = self.valid + self.tiles
        self.second = self.first + count
        self.me = self.second + count
        self.size = self.me + 1


def start_of(table, lay, pos):
    start = jnp.zeros_like(pos)
    for r in range(lay.reqs - 1):
        end = table[lay.ends + r]
        start = jnp.where(pos >= end, end, start)
    return start


def attend(table, lay, heads, scale, source, chunk, query, keys, values, peak, total, accum):
    half = lay.rows // 2
    row0 = chunk * TILE
    base1, base2 = table[lay.first + source], table[lay.second + source] - half
    row = row0 + lax.broadcasted_iota(jnp.int32, (1, TILE), 1)
    pos = jnp.where(row < half, base1, base2) + row
    start = start_of(table, lay, pos)
    row1 = row0 + TILE
    pieces = (
        (base1 + jnp.minimum(row0, half), base1 + jnp.minimum(row1, half)),
        (base2 + jnp.maximum(row0, half), base2 + jnp.maximum(row1, half)),
    )
    begins = [start_of(table, lay, low) for low, _ in pieces]
    peak[...] = jnp.full_like(peak, LOWEST)
    total[...] = jnp.zeros_like(total)
    accum[...] = jnp.zeros_like(accum)

    def tile(t, _):
        spans = ((table[lay.low + t], table[lay.high + t]), (table[lay.low2 + t], table[lay.high2 + t]))
        live = table[lay.valid + t]
        fresh_key = t < lay.chunks
        used = False
        for (low, high), begin in zip(pieces, begins):
            from_here = jnp.where(fresh_key, begin, low)
            for key_low, key_high in spans:
                used = used | ((low < high) & (key_low < key_high) & (from_here < key_high) & (key_low < high))

        @pl.when(used)
        def _():
            key = lax.broadcasted_iota(jnp.int32, (TILE, TILE), 0)
            length = spans[0][1] - spans[0][0]
            shift1 = jnp.where(fresh_key, spans[0][0], 0)
            shift2 = jnp.where(fresh_key, spans[1][0] - length, 0)
            key = key + jnp.where(key < length, shift1, shift2)
            limit = jnp.where((pos >= spans[0][0]) & (pos < spans[0][1]), live, 0) - 1
            low = jnp.where(fresh_key, start, 0)
            high = jnp.where(fresh_key, pos, limit)
            visible = (key >= low) & (key <= high)
            for h in range(heads):
                cols = slice(h * HEAD_DIM, (h + 1) * HEAD_DIM)
                scores = lax.dot_general(
                    keys[t, :, cols], query[cols], (((1,), (1,)), ((), ())), preferred_element_type=jnp.float32
                )
                scores = jnp.where(visible, scores * scale, -jnp.inf)
                old = peak[h : h + 1]
                fresh = jnp.maximum(old, jnp.max(scores, axis=0, keepdims=True))
                weights = jnp.exp2(scores - fresh)
                factor = jnp.exp2(old - fresh)
                peak[h : h + 1] = fresh
                total[h : h + 1] = total[h : h + 1] * factor + jnp.sum(weights, axis=0, keepdims=True)
                accum[cols] = accum[cols] * factor + jnp.dot(
                    values[t, cols], weights.astype(jnp.bfloat16), preferred_element_type=jnp.float32
                )

        return 0

    lax.fori_loop(0, lay.tiles, tile, 0)


def put_level(item, feat, heads, level):
    high = level.astype(jnp.bfloat16).astype(jnp.float32)
    rest = level - high
    middle = rest.astype(jnp.bfloat16).astype(jnp.float32)
    parts = [high, middle, rest - middle, jnp.zeros((TAIL - 3 * heads, TILE), jnp.float32)]
    item[feat : feat + TAIL] = jnp.concatenate(parts, axis=0).astype(jnp.bfloat16)


def level_of(item, feat, heads):
    tail = item[feat : feat + TAIL].astype(jnp.float32)
    return tail[:heads] + tail[heads : 2 * heads] + tail[2 * heads : 3 * heads]


def settle(heads, peak, total, accum, item):
    sums = total[:heads]
    empty = sums == 0.0
    safe = jnp.where(empty, 1.0, sums)
    level = jnp.where(empty, FLOOR, peak[:heads] + jnp.log2(safe))
    inverse = 1.0 / safe
    for h in range(heads):
        cols = slice(h * HEAD_DIM, (h + 1) * HEAD_DIM)
        item[cols] = (accum[cols] * inverse[h : h + 1]).astype(jnp.bfloat16)
    put_level(item, heads * HEAD_DIM, heads, level)


def merge(heads, items, out):
    feat = heads * HEAD_DIM
    levels = [level_of(item, feat, heads) for item in items]
    top = functools.reduce(jnp.maximum, levels)
    total = sum(jnp.exp2(level - top) for level in levels)
    level = top + jnp.log2(total)
    shares = [jnp.exp2(one - level) for one in levels]
    for h in range(heads):
        cols = slice(h * HEAD_DIM, (h + 1) * HEAD_DIM)
        value = sum(item[cols].astype(jnp.float32) * share[h : h + 1] for item, share in zip(items, shares))
        out(h, cols, value)
    return level


def merge_item(heads, items, item):
    def out(h, cols, value):
        item[cols] = value.astype(jnp.bfloat16)

    put_level(item, heads * HEAD_DIM, heads, merge(heads, items, out))


def pack_kernel(heads, chunks, queries, *items):
    for c in range(chunks):
        for h in range(heads):
            cols = slice(h * HEAD_DIM, (h + 1) * HEAD_DIM)
            items[c][cols] = queries[c * TILE : (c + 1) * TILE, cols]
        items[c][heads * HEAD_DIM :] = jnp.zeros((TAIL, TILE), jnp.bfloat16)


def first_kernel(lay, heads, scale, me_ref, pos_ref, span_len, prefix_len, blocks, span, pool, *refs):
    queries, (table, keys, values), own = refs[: lay.chunks], refs[lay.chunks : lay.chunks + 3], refs[lay.chunks + 3 : -4]
    query, peak, total, accum = refs[-4:]
    me = me_ref[0]
    reqs, most = blocks.shape[0], blocks.shape[1]
    width = pool.shape[2]
    rows, half = lay.rows, lay.rows // 2
    begins, end = [], jnp.int32(0)
    for r in range(reqs):
        begins.append(end)
        end = end + span_len[r]
        table[lay.ends + r] = end
    for b in range(lay.count):
        table[lay.first + b] = pos_ref[b * rows]
        table[lay.second + b] = pos_ref[b * rows + half]
    table[lay.me] = me
    base1, base2 = pos_ref[me * rows], pos_ref[me * rows + half] - half
    for t in range(lay.chunks):
        low, high = t * TILE, (t + 1) * TILE
        spans = [(base + max(low, a), base + min(high, b)) for a, b, base in ((0, half, base1), (half, rows, base2)) if max(low, a) < min(high, b)]
        if len(spans) == 1:
            spans.append((jnp.int32(0), jnp.int32(0)))
        for place, number in zip((lay.low, lay.high, lay.low2, lay.high2), spans[0] + spans[1]):
            table[place + t] = number
        table[lay.valid + t] = 0
    for t in range(lay.chunks, lay.tiles):
        table[lay.low2 + t] = 0
        table[lay.high2 + t] = 0
    for r in range(reqs):
        for b in range(most):

            @pl.when(blocks[r, b, 0] == me)
            def _():
                t = lay.chunks + blocks[r, b, 1]
                live = jnp.clip(prefix_len[r] - b * width, 0, width)
                table[lay.low + t] = begins[r]
                table[lay.high + t] = jnp.where(live > 0, table[lay.ends + r], begins[r])
                table[lay.valid + t] = live

    for t in range(lay.chunks):
        keys[t] = span[0, t * TILE : (t + 1) * TILE]
        for h in range(heads):
            cols = slice(h * HEAD_DIM, (h + 1) * HEAD_DIM)
            values[t, cols] = span[1, t * TILE : (t + 1) * TILE, cols].T
    for slot in range(lay.slots):
        keys[lay.chunks + slot] = pool[slot, 0]
        for h in range(heads):
            cols = slice(h * HEAD_DIM, (h + 1) * HEAD_DIM)
            values[lay.chunks + slot, cols] = pool[slot, 1, :, cols].T

    def one(c, _):
        for fixed in range(lay.chunks):

            @pl.when(c == fixed)
            def _():
                query[...] = queries[fixed][...]

        attend(table, lay, heads, scale, me, c, query, keys, values, peak, total, accum)
        for fixed in range(lay.chunks):

            @pl.when(c == fixed)
            def _():
                settle(heads, peak, total, accum, own[fixed])

        return 0

    lax.fori_loop(0, lay.chunks, one, 0)


def side(me, block):
    return block + 1 - 2 * lax.rem(block, 2)


def step_kernel(lay, heads, scale, chunk, step, table, *refs):
    refs, (query, peak, total, accum) = refs[:-4], refs[-4:]
    me = table[lay.me]
    end = (me == 0) | (me == lay.count - 1)
    middle = jnp.logical_not(end)
    across = lay.count - 1 - me
    if step == 1:
        got, other, keys, values, out, keep = refs
        mine, source = got, side(me, me)
    else:
        got, held, other, keys, values, out, keep = refs
        mine = query
        pick = jnp.where(end, 1, 0) if step == 2 else jnp.where(end, 0, 1)
        source = jnp.where(pick == 1, side(me, across), across)

        @pl.when(end)
        def _():
            query[...] = got[...]

        @pl.when(middle)
        def _():
            query[...] = held[...]

    @pl.when(middle)
    def _():
        if step == 3:
            merge_item(heads, (got, other), out)
        else:
            out[...] = other[...]

    attend(table, lay, heads, scale, source, chunk, mine, keys, values, peak, total, accum)

    @pl.when(end)
    def _():
        settle(heads, peak, total, accum, out)

    @pl.when(middle)
    def _():
        settle(heads, peak, total, accum, keep)


def join_kernel(lay, heads, table, got, kept, *refs):
    out = refs[-1]
    me = table[lay.me]
    end = (me == 0) | (me == lay.count - 1)

    @pl.when(jnp.logical_not(end))
    def _():
        merge_item(heads, (got, kept), out)

    if len(refs) == 2:

        @pl.when(end)
        def _():
            out[...] = refs[0][...]


def finish_kernel(lay, heads, chunk, table, own, from_side, from_middle, to_end, *refs):
    out, turned, sem = refs[-3:]
    me = table[lay.me]
    end = (me == 0) | (me == lay.count - 1)

    def put(h, cols, value):
        turned[:, cols] = value.T.astype(jnp.bfloat16)

    @pl.when(end)
    def _():
        merge(heads, (own, to_end), put)

    @pl.when(jnp.logical_not(end))
    def _():
        merge(heads, (own, from_side, from_middle), put)

    copy = pltpu.make_async_copy(turned, out.at[0, pl.ds(chunk * TILE, TILE)], sem)
    copy.start()
    copy.wait()


def hop_kernel(lay, heads, scale, chunk, distance, table, query_left, query_right, keys, values, *refs):
    refs, (kept, peak, total, accum) = refs[:-4], refs[-4:]
    me = table[lay.me]
    out_left, out_right = refs[-2:]
    got_left, got_right = refs[:2] if len(refs) == 4 else (None, None)
    for query, got, out, source, more in (
        (query_left, got_left, out_left, me - distance, me + 1 < lay.count),
        (query_right, got_right, out_right, me + distance, me > 0),
    ):

        @pl.when((source >= 0) & (source < lay.count))
        def _():
            attend(table, lay, heads, scale, source, chunk, query, keys, values, peak, total, accum)
            if got is None:
                settle(heads, peak, total, accum, out)
            else:
                settle(heads, peak, total, accum, kept)

                @pl.when(more)
                def _():
                    merge_item(heads, (kept, got), out)

                @pl.when(jnp.logical_not(more))
                def _():
                    out[...] = kept[...]


def hop_finish_kernel(lay, heads, chunk, table, own, from_left, from_right, *refs):
    out, turned, sem = refs[-3:]
    me = table[lay.me]

    def put(h, cols, value):
        turned[:, cols] = value.T.astype(jnp.bfloat16)

    @pl.when(me == 0)
    def _():
        merge(heads, (own, from_right), put)

    @pl.when(me == lay.count - 1)
    def _():
        merge(heads, (own, from_left), put)

    @pl.when((me > 0) & (me < lay.count - 1))
    def _():
        merge(heads, (own, from_left, from_right), put)

    copy = pltpu.make_async_copy(turned, out.at[0, pl.ds(chunk * TILE, TILE)], sem)
    copy.start()
    copy.wait()


def shards(queries, span_kv, prefix_pool, token_pos, span_lens, prefix_lens, block_table):
    rows, feat = queries.shape[1], queries.shape[2]
    heads = feat // HEAD_DIM
    count = lax.axis_size("ctx") // HGROUPS
    slots, width = prefix_pool.shape[1], prefix_pool.shape[3]
    assert width == TILE and rows % TILE == 0
    scale = LOG2E / math.sqrt(HEAD_DIM)
    lay = Layout(span_lens.shape[0], rows, slots, count)
    chunks, tiles = lay.chunks, lay.tiles
    me = (lax.axis_index("ctx") // HGROUPS).reshape(1)

    smem = pl.BlockSpec(memory_space=pltpu.SMEM)
    vmem = pl.BlockSpec(memory_space=pltpu.VMEM)
    anywhere = pl.BlockSpec(memory_space=pl.ANY)
    item = jax.ShapeDtypeStruct((feat + TAIL, TILE), jnp.bfloat16)
    state = [
        pltpu.VMEM(item.shape, item.dtype),
        pltpu.VMEM((8, TILE), jnp.float32),
        pltpu.VMEM((8, TILE), jnp.float32),
        pltpu.VMEM((feat, TILE), jnp.float32),
    ]
    params = pltpu.CompilerParams(vmem_limit_bytes=16 * 1024 * 1024)

    def cost(blocks):
        return pl.CostEstimate(
            flops=blocks * 4 * TILE * tiles * TILE * feat,
            bytes_accessed=tiles * 4 * TILE * feat,
            transcendentals=blocks * tiles * TILE * TILE * heads,
        )

    light = pl.CostEstimate(flops=8 * TILE * feat, bytes_accessed=8 * TILE * feat, transcendentals=0)

    def call(kernel, name, args, outs, cost_estimate, scratch=()):
        return pl.pallas_call(
            kernel,
            out_shape=[item] * outs,
            in_specs=[smem] + [vmem] * (len(args) - 1),
            out_specs=[vmem] * outs,
            scratch_shapes=list(scratch),
            compiler_params=params,
            cost_estimate=cost_estimate,
            name=name,
        )(*args)

    def finish(kernel, c, args, out):
        given = () if out is None else (out,)
        return pl.pallas_call(
            functools.partial(kernel, lay, heads, c),
            out_shape=jax.ShapeDtypeStruct(queries.shape, queries.dtype),
            in_specs=[smem] + [vmem] * (len(args) - 1) + [anywhere] * len(given),
            out_specs=anywhere,
            scratch_shapes=[pltpu.VMEM((TILE, feat), jnp.bfloat16), pltpu.SemaphoreType.DMA],
            input_output_aliases={len(args): 0} if given else {},
            compiler_params=params,
            cost_estimate=light,
            name="finish",
        )(*args, *given)

    query = pl.pallas_call(
        functools.partial(pack_kernel, heads, chunks),
        out_shape=[item] * chunks,
        in_specs=[vmem],
        out_specs=[vmem] * chunks,
        compiler_params=params,
        cost_estimate=light,
        name="pack",
    )(queries[0])
    table, keys, values, *own = pl.pallas_call(
        functools.partial(first_kernel, lay, heads, scale),
        out_shape=[
            jax.ShapeDtypeStruct((lay.size,), jnp.int32),
            jax.ShapeDtypeStruct((tiles, TILE, feat), jnp.bfloat16),
            jax.ShapeDtypeStruct((tiles, feat, TILE), jnp.bfloat16),
        ]
        + [item] * chunks,
        in_specs=[smem] * 5 + [vmem] * (2 + chunks),
        out_specs=[smem] + [vmem] * (2 + chunks),
        scratch_shapes=state,
        compiler_params=params,
        cost_estimate=cost(chunks),
        name="own_part",
    )(me, token_pos, span_lens, prefix_lens, block_table, span_kv[0], prefix_pool[0], *query)

    if count == 4:
        out = along_four(lay, heads, scale, table, keys, values, query, own, call, finish, cost(1), light, state)
    else:
        out = along_line(lay, heads, scale, table, keys, values, query, own, call, finish, cost(1), state)
    return out


def along_four(lay, heads, scale, table, keys, values, query, own, call, finish, heavy, light, state):
    count, chunks = lay.count, lay.chunks
    each = range(chunks)

    def swap_a(value):
        return send(value, lambda block: block ^ 1, count)

    def swap_b(value):
        return send(value, lambda block: block if block in (0, count - 1) else count - 1 - block, count)

    def step(number, c, *args):
        kernel = functools.partial(step_kernel, lay, heads, scale, c, number)
        return call(kernel, "step%d" % number, (table, *args, keys, values), 2, heavy, state)

    def join(*args):
        return call(functools.partial(join_kernel, lay, heads), "join", (table, *args), 1, light)[0]

    a1 = [swap_a(query[c]) for c in each]
    b1 = [swap_b(query[c]) for c in each]
    b2 = [swap_b(a1[c]) for c in each]
    sent, kept1 = zip(*(step(1, c, a1[c], b1[c]) for c in each))
    a2 = [swap_a(sent[c]) for c in each]
    sent, kept2 = zip(*(step(2, c, a2[c], b1[c], b2[c]) for c in each))
    a3 = [swap_a(sent[c]) for c in each]
    sent, kept3 = zip(*(step(3, c, a3[c], b2[c], kept2[c]) for c in each))
    b3 = [swap_b(sent[c]) for c in each]
    lag = 2
    home, back = [None] * chunks, [None] * chunks
    for c in range(chunks + lag):
        value = sent[c] if c < chunks else None
        if c >= lag:
            value = join(back[c - lag], kept1[c - lag], *(() if value is None else (value,)))
        got = swap_a(value)
        if c >= lag:
            home[c - lag] = got
        if c < chunks:
            back[c] = swap_b(join(got, kept3[c]))
    out = None
    for c in each:
        out = finish(finish_kernel, c, (table, own[c], a2[c], b3[c], home[c]), out)
    return out


def along_line(lay, heads, scale, table, keys, values, query, own, call, finish, heavy, state):
    count = lay.count

    def hop(value, right, first, last):
        step = 1 if right else -1
        return send(value, lambda block: block + step if first <= block < last else None, count)

    out = None
    for c in range(lay.chunks):
        left, right = [query[c]], [query[c]]
        for d in range(1, count):
            left.append(hop(left[-1], True, d - 1, count - 1))
            right.append(hop(right[-1], False, 1, count - d + 1))
        got = ()
        for d in range(count - 1, 0, -1):
            kernel = functools.partial(hop_kernel, lay, heads, scale, c, d)
            items = call(kernel, "hop", (table, left[d], right[d], keys, values, *got), 2, heavy, state)
            got = (hop(items[0], False, d, count), hop(items[1], True, 0, count - d))
        out = finish(hop_finish_kernel, c, (table, own[c], got[1], got[0]), out)
    return out


def solution(mesh):
    placed = (
        P(("groups", "ctx"), None, None),
        P(("groups", "ctx"), None, None, None),
        P(("groups", "ctx"), None, None, None, None),
        P("groups"),
        P("groups"),
        P("groups"),
        P("groups", None, None),
    )
    return jax.shard_map(
        shards,
        mesh=mesh,
        in_specs=placed,
        out_specs=P(("groups", "ctx"), None, None),
        check_vma=False,
    )
```
